32 devices in a mesh: groups: 2 (over y), seq: 4 (over z), dp: 2 (over x), tensor: 2 (over core).
Axes of the slice: x: 2, y: 2, z: 4, core: 2. Of those that a mesh axis runs over, the one named last changes fastest.
Arguments:
- queries: bfloat16 [4, 768, 1024], P(('groups', 'dp'), 'seq', 'tensor'), parts along dimension 0, may hold values from -80 to 80
- key_rows: bfloat16 [4, 768, 1024], P(('groups', 'dp'), 'seq', 'tensor'), parts along dimension 0, may hold values from -80 to 80
- value_rows: bfloat16 [4, 768, 1024], P(('groups', 'dp'), 'seq', 'tensor'), parts along dimension 0, may hold values from -6 to 6
- utterance: int32 [4, 768], P(('groups', 'dp'), 'seq'), parts along dimension 0, may hold values from 0 to 7, never falling along the last dimension, each value on 1 to 576 neighbouring positions
- cotangent: bfloat16 [4, 768, 1024], P(('groups', 'dp'), 'seq'), parts along dimension 0, may hold values from -6 to 6
- out_weight: bfloat16 [1024, 1024], P('tensor'), may hold values from -0.1875 to 0.1875
Outputs:
- grad_queries: bfloat16 [4, 768, 1024], P(('groups', 'dp'), 'seq', 'tensor'), parts along dimension 0
- grad_keys: bfloat16 [4, 768, 1024], P(('groups', 'dp'), 'seq', 'tensor'), parts along dimension 0
- grad_values: bfloat16 [4, 768, 1024], P(('groups', 'dp'), 'seq', 'tensor'), parts along dimension 0
- grad_out_weight: float32 [2048, 1024], P(('groups', 'tensor')), parts along dimension 0
The draws below stay inside these ranges and needn't reach their ends.
There are 2 independent parts, one for each index of `groups`. The reference program is written for one: setup_inputs(seed, part) draws one part's arguments, and reference() takes and returns one part's arrays. A program takes and returns all parts, laid end to end along the dimension named above; an argument that names none is the same for every part. Nothing has to cross between parts.
Inputs may be any that keep to these rules, and one draw needn't show every extreme that they name: Within each packed sequence utterance numbers never fall, all 8 occur, each utterance spans 1 to 576 frames and one spans exactly 576.
All inputs are finite; a program needn't handle non-finite values.
Results may differ from the reference program's by a relative error of at most 0.02.
Values may be sent and summed in bfloat16 or wider, within the bound.
A program may use at most 128 MiB of HBM per device.

```python
import math
import jax
import jax.numpy as jnp
import numpy as np
from jax import lax

D = 1024
HEADS = 16
HD = 64
UTTS = 8
FRAMES = 768
SEQS = 2
UTT_MOST = 576


def paired_rows(key):
    shape = (SEQS, FRAMES, D)
    base_keys = jnp.clip(jax.random.normal(jax.random.fold_in(key, 101), shape, jnp.float32), -6.0, 6.0)
    base_queries = jnp.clip(jax.random.normal(jax.random.fold_in(key, 202), shape, jnp.float32), -6.0, 6.0)
    return (base_queries, base_keys)


def draw_queries(key, part):
    return paired_rows(key)[0].astype(jnp.bfloat16)


def draw_key_rows(key, part):
    return paired_rows(key)[1].astype(jnp.bfloat16)


def levels(rng, shape, shards, least, top_value):
    loudness, own = 1.0, jax.random.fold_in(rng, 6)
    for position, shards_of in shards:
        steps = jnp.exp(jax.random.uniform(jax.random.fold_in(own, position), (shards_of,), jnp.float32, least / len(shards), top_value / len(shards)))
        loudness = loudness * jnp.repeat(steps, shape[position] // shards_of).reshape([-1 if axis == position else 1 for axis in range(len(shape))])
    return loudness


def length_profile(amount, total, limit, skew):
    loads = [(1 << 20) // math.isqrt(grade ** skew) + 1 for grade in range(2, amount + 1)]
    spare, counts = total - limit - (amount - 1), [1] * (amount - 1)
    while spare > 0:
        free = [i for i in range(amount - 1) if counts[i] < limit]
        whole, budget = sum([loads[i] for i in free]), spare
        for i in free:
            more = min(limit - counts[i], max(1, budget * loads[i] // whole), spare)
            counts[i] = counts[i] + more
            spare = spare - more
    return np.array([limit] + counts)


def ragged(key, count, total, limit, lean):
    if count == 2:
        one = jax.random.randint(key, (), max(1, total - limit), min(limit, total - 1) + 1)
        return jnp.stack([one, total - one])
    tallies = jnp.asarray(length_profile(count, total, limit, lean), jnp.int32)
    pairs = (count - 1) // 2
    donor, taker = tallies[1:1 + 2 * pairs:2], tallies[2:2 + 2 * pairs:2]
    slack = jnp.minimum(donor - 1, limit - taker)
    moved = jax.random.randint(jax.random.fold_in(key, 1), (pairs,), 0, 1 << 20) % (slack + 1)
    tallies = tallies.at[1:1 + 2 * pairs:2].set(donor - moved).at[2:2 + 2 * pairs:2].set(taker + moved)
    return tallies[jax.random.permutation(jax.random.fold_in(key, 2), count)]


def centred(stream_key, extent, deviation, bound, cuts=(), kind=jnp.bfloat16):
    loudness = levels(stream_key, extent, cuts, -0.22, 0.18) if cuts else 1.0
    drawn = jax.random.normal(stream_key, extent, jnp.float32) * deviation * loudness
    return jnp.minimum(jnp.maximum(drawn, -bound), bound).astype(kind)


def setup_inputs(seed: int = 0, part: int = 0) -> dict:
    key_list = jax.random.split(jax.random.key(seed), 7)
    part_keys = jax.random.split(jax.random.fold_in(key_list[6], part), 7)
    queries = draw_queries(jax.random.fold_in(jax.random.fold_in(key_list[6], part), 71), part)
    key_rows = draw_key_rows(jax.random.fold_in(jax.random.fold_in(key_list[6], part), 71), part)
    value_rows = centred(part_keys[2], (SEQS, FRAMES, D), 1.0, 6.0, ((0, 2), (1, 4), (2, 2)))
    utterance = jax.vmap(lambda own: jnp.searchsorted(jnp.cumsum(ragged(own, UTTS, FRAMES, UTT_MOST, 2)), jnp.arange(FRAMES), side="right"))(jax.random.split(part_keys[3], SEQS)).reshape((SEQS, FRAMES)).astype(jnp.int32)
    cotangent = centred(part_keys[4], (SEQS, FRAMES, D), 1.0, 6.0, ((0, 2), (1, 4)))
    out_weight = centred(key_list[5], (D, D), D ** -0.5, 0.1875, ((0, 2),))
    return {"queries": queries, "key_rows": key_rows, "value_rows": value_rows, "utterance": utterance, "cotangent": cotangent, "out_weight": out_weight}


MASKED_SCORE = -1.0e30


def to_heads(array):
    return array.reshape(SEQS, FRAMES, HEADS, HD).transpose(0, 2, 1, 3).reshape(SEQS * HEADS, FRAMES, HD)


def from_heads(array):
    return array.reshape(SEQS, HEADS, FRAMES, HD).transpose(0, 2, 1, 3).reshape(SEQS, FRAMES, D)


def per_head(item_tuple):
    query_h, key_h, value_h, dout_h, utt_ids = item_tuple
    scale = HD ** -0.5
    scores = jnp.dot(query_h, key_h.T, preferred_element_type=jnp.float32) * scale
    same_utt = utt_ids[:, None] == utt_ids[None, :]
    scores = jnp.where(same_utt, scores, MASKED_SCORE)
    row_max = jnp.max(scores, axis=1, keepdims=True)
    log_norm = row_max + jnp.log(jnp.sum(jnp.exp(scores - row_max), axis=1, keepdims=True))
    probs = jnp.exp(scores - log_norm)
    probs_low = probs.astype(jnp.bfloat16)
    attended = jnp.dot(probs_low, value_h, preferred_element_type=jnp.float32).astype(jnp.bfloat16)
    row_delta = jnp.sum(dout_h.astype(jnp.float32) * attended.astype(jnp.float32), axis=1, keepdims=True)
    prob_grads = jnp.dot(dout_h, value_h.T, preferred_element_type=jnp.float32)
    score_grads = (probs * (prob_grads - row_delta) * scale).astype(jnp.bfloat16)
    grad_query = jnp.dot(score_grads, key_h, preferred_element_type=jnp.float32).astype(jnp.bfloat16)
    grad_key = jnp.dot(score_grads.T, query_h, preferred_element_type=jnp.float32).astype(jnp.bfloat16)
    grad_value = jnp.dot(probs_low.T, dout_h, preferred_element_type=jnp.float32).astype(jnp.bfloat16)
    return attended, grad_query, grad_key, grad_value


def reference(queries, key_rows, value_rows, utterance, cotangent, out_weight):
    flat_cot = cotangent.reshape(SEQS * FRAMES, D)
    d_attended = lax.dot_general(flat_cot, out_weight, (((1,), (1,)), ((), ())), preferred_element_type=jnp.float32).astype(jnp.bfloat16)
    d_attended = d_attended.reshape(SEQS, FRAMES, D)
    utt_heads = jnp.repeat(utterance, HEADS, axis=0)
    attended, grad_query, grad_key, grad_value = lax.map(per_head, (to_heads(queries), to_heads(key_rows), to_heads(value_rows), to_heads(d_attended), utt_heads))
    attended_flat = from_heads(attended).reshape(SEQS * FRAMES, D)
    grad_weight = jnp.dot(attended_flat.T, flat_cot, preferred_element_type=jnp.float32)
    return from_heads(grad_query), from_heads(grad_key), from_heads(grad_value), grad_weight
```

```python
import functools
import math

import jax
import jax.numpy as jnp
from jax import lax
from jax.experimental import pallas as pl
from jax.experimental.pallas import tpu as pltpu
from jax.sharding import PartitionSpec as P

HD = 64


MASKED_SCORE = -1e30


def heads_of(array):
    return array.reshape(array.shape[0], array.shape[1] // HD, HD)


def block_scores(query_block, key_block, query_utts, key_utts):
    scores = jnp.einsum(
        "qhd,khd->hqk", query_block, key_block, preferred_element_type=jnp.float32
    ) * HD ** (-0.5)
    same_utt = query_utts[:, None] == key_utts[None, :]
    return jnp.where(same_utt[None], scores, MASKED_SCORE)


def score_gradient(probs, dout_block, value_block, delta_rows):
    prob_grads = jnp.einsum(
        "qhd,khd->hqk", dout_block, value_block, preferred_element_type=jnp.float32
    )
    return (probs * (prob_grads - delta_rows[:, :, None]) * HD ** (-0.5)).astype(jnp.bfloat16)


def local(queries, key_rows, value_rows, utterance, cotangent, out_weight):
    own_queries = queries[0]
    frames_dev = own_queries.shape[0]
    width_dev = own_queries.shape[1]
    heads_dev = width_dev // HD
    query_heads = heads_of(own_queries)
    my_utts = utterance[0]
    utts_all = lax.all_gather(my_utts, "seq", axis=0, tiled=True)
    keys_all, values_all = (
        lax.all_gather(key_rows[0], "seq", axis=0, tiled=True),
        lax.all_gather(value_rows[0], "seq", axis=0, tiled=True),
    )
    frames_all = keys_all.shape[0]
    key_span = math.gcd(frames_all, 512)
    block_count = frames_all // key_span

    def key_block(block_index):
        offset = block_index * key_span
        key_block_rows = heads_of(lax.dynamic_slice_in_dim(keys_all, offset, key_span, 0))
        value_block_rows = heads_of(lax.dynamic_slice_in_dim(values_all, offset, key_span, 0))
        utt_block = lax.dynamic_slice_in_dim(utts_all, offset, key_span, 0)
        return (key_block_rows, value_block_rows, utt_block)

    def stats_step(block_index, carried):
        key_block_rows, value_block_rows, utt_block = key_block(block_index)
        running_max, running_sum = carried
        scores = block_scores(query_heads, key_block_rows, my_utts, utt_block)
        new_max = jnp.maximum(running_max, jnp.max(scores, axis=2))
        running_sum = running_sum * jnp.exp(running_max - new_max) + jnp.sum(
            jnp.exp(scores - new_max[:, :, None]), axis=2
        )
        return (new_max, running_sum)

    start_max = jnp.full((heads_dev, frames_dev), MASKED_SCORE, jnp.float32)
    start_sum = jnp.zeros((heads_dev, frames_dev), jnp.float32)
    running_max, running_sum = lax.fori_loop(0, block_count, stats_step, (start_max, start_sum))
    log_norm = running_max + jnp.log(running_sum)

    def output_step(block_index, carried):
        key_block_rows, value_block_rows, utt_block = key_block(block_index)
        scores = block_scores(query_heads, key_block_rows, my_utts, utt_block)
        probs_low = jnp.exp(scores - log_norm[:, :, None]).astype(jnp.bfloat16)
        return carried + jnp.einsum(
            "hqk,khd->hqd", probs_low, value_block_rows, preferred_element_type=jnp.float32
        )

    head_zeros = jnp.zeros((heads_dev, frames_dev, HD), jnp.float32)
    attended_acc = lax.fori_loop(0, block_count, output_step, head_zeros)
    attended = attended_acc.transpose(1, 0, 2).reshape(frames_dev, width_dev).astype(jnp.bfloat16)
    own_cot = cotangent[0]
    d_attended = lax.dot_general(
        own_cot, out_weight, (((1,), (1,)), ((), ())), preferred_element_type=jnp.float32
    ).astype(jnp.bfloat16)
    weight_term = lax.dot_general(
        attended, own_cot, (((0,), (0,)), ((), ())), preferred_element_type=jnp.float32
    )
    grad_weight = lax.psum(weight_term, ("seq", "dp"))
    dout_heads = heads_of(d_attended)
    row_delta = jnp.einsum(
        "qhd,qhd->hq", dout_heads.astype(jnp.float32), heads_of(attended).astype(jnp.float32)
    )

    def joint_step(block_index, carried):
        key_block_rows, value_block_rows, utt_block = key_block(block_index)
        query_acc_now, buffer = carried
        scores = block_scores(query_heads, key_block_rows, my_utts, utt_block)
        probs = jnp.exp(scores - log_norm[:, :, None])
        score_grads = score_gradient(probs, dout_heads, value_block_rows, row_delta)
        query_acc_now = query_acc_now + jnp.einsum(
            "hqk,khd->hqd", score_grads, key_block_rows, preferred_element_type=jnp.float32
        )
        key_part = jnp.einsum(
            "hqk,qhd->khd", score_grads, query_heads, preferred_element_type=jnp.float32
        )
        value_part = jnp.einsum(
            "hqk,qhd->khd",
            probs.astype(jnp.bfloat16),
            dout_heads,
            preferred_element_type=jnp.float32,
        )
        joined = jnp.concatenate(
            [key_part.reshape(key_span, width_dev), value_part.reshape(key_span, width_dev)], axis=1
        )
        buffer = lax.dynamic_update_slice_in_dim(buffer, joined, block_index * key_span, 0)
        return (query_acc_now, buffer)

    term_zeros = jnp.zeros((frames_all, 2 * width_dev), jnp.float32)
    query_acc, terms_all = lax.fori_loop(0, block_count, joint_step, (head_zeros, term_zeros))
    summed = lax.psum_scatter(terms_all, "seq", scatter_dimension=0, tiled=True)
    grad_key = summed[:, :width_dev].astype(jnp.bfloat16)
    grad_value = summed[:, width_dev:].astype(jnp.bfloat16)
    grad_query = query_acc.transpose(1, 0, 2).reshape(frames_dev, width_dev).astype(jnp.bfloat16)
    return (grad_query[None], grad_key[None], grad_value[None], grad_weight)


PAIR = 2 * HD
NT = (((1,), (1,)), ((), ()))
TN = (((0,), (0,)), ((), ()))
MESH = pl.DeviceIdType.MESH


def dot(a, b, dims=(((1,), (0,)), ((), ()))):
    return lax.dot_general(a, b, dims, preferred_element_type=jnp.float32)


def fused_kernel(
    n, q_ref, k_ref, v_ref, utt_ref, cot_ref, w_ref,
    dq_ref, dk_ref, dv_ref, gw_ref,
    q_all, k_all, v_all, utt_all, cot_all, utt_col, utt_row, probs_all, att_all, dout_all,
    dq_all, dk_all, dv_all, dk_acc, dv_acc, gw_part, gw_send, gw_recv,
    in_send, in_recv, cot_send, cot_recv, core_send, core_recv,
    out_send, out_recv, pair_send, pair_recv, gz_send, gz_recv, gx_send, gx_recv,
):
    me = lax.axis_index("seq")
    core = lax.axis_index("tensor")
    side = lax.axis_index("dp")
    rows = q_ref.shape[0]
    depth = cot_ref.shape[1]
    half = depth // 2
    scale = HD ** -0.5

    def peer(d):
        return lax.rem(me + d, n)

    def source(d):
        return lax.rem(me + n - d, n)

    def frames(s):
        return pl.ds(pl.multiple_of(s * rows, rows), rows)

    def pair(s):
        return pl.ds(pl.multiple_of(s * PAIR, PAIR), PAIR)

    def halfcols(s):
        return pl.ds(pl.multiple_of(s * half, half), half)

    def remote(src, dst, ssem, rsem, target):
        return pltpu.make_async_remote_copy(
            src_ref=src, dst_ref=dst, send_sem=ssem, recv_sem=rsem,
            device_id=target, device_id_type=MESH,
        )

    barrier = pltpu.get_barrier_semaphore()
    for d in range(1, n):
        pl.semaphore_signal(barrier, inc=1, device_id={"seq": peer(d)}, device_id_type=MESH)
    pl.semaphore_signal(barrier, inc=1, device_id={"tensor": 1 - core}, device_id_type=MESH)
    pl.semaphore_signal(barrier, inc=1, device_id={"dp": 1 - side}, device_id_type=MESH)
    pl.semaphore_wait(barrier, n + 1)

    in_copies = []
    for d in range(1, n):
        to = {"seq": peer(d)}
        cols = pair(peer(d))
        in_copies.append(remote(utt_ref, utt_all.at[me], in_send.at[3, d], in_recv.at[3, d], to))
        for t, (src, dst) in enumerate(((k_ref, k_all), (v_ref, v_all), (q_ref, q_all))):
            in_copies.append(remote(
                src.at[:, cols], dst.at[frames(me), :], in_send.at[t, d], in_recv.at[t, d], to))
    for copy in in_copies:
        copy.start()
    cot_copies = []
    for d in range(1, n):
        cot_copies.append(remote(
            cot_ref.at[:, halfcols(core)], cot_all.at[frames(me), halfcols(core)],
            cot_send.at[d], cot_recv.at[d], {"seq": peer(d)}))
        cot_copies[-1].start()

    own = pair(me)
    q_all[frames(me), :] = q_ref[:, own]
    k_all[frames(me), :] = k_ref[:, own]
    v_all[frames(me), :] = v_ref[:, own]
    cot_all[frames(me), :] = cot_ref[...]
    utt_all[me] = utt_ref[...]
    for copy in in_copies:
        copy.wait_recv()

    for s in range(n):
        wide = jnp.broadcast_to(utt_all[s, 0:1, :], (128, utt_all.shape[2]))
        utt_col[s * rows:(s + 1) * rows, :] = jnp.transpose(wide)[:rows, :]
    utt_row[...] = jnp.transpose(utt_col[...])[0:8, :]

    lane = lax.broadcasted_iota(jnp.int32, (rows, PAIR), 1)
    first = lane < HD
    masks = [first.astype(jnp.float32), (lane >= HD).astype(jnp.float32)]
    masks_low = [m.astype(jnp.bfloat16) for m in masks]

    def forward(i, carry):
        here = frames(i)
        q = q_all[here, :]
        same = utt_col[here, 0:1] == utt_row[0:1, :]
        outs = []
        for h in range(2):
            scores = dot(q * masks_low[h], k_all[...], NT) * scale
            scores = jnp.where(same, scores, MASKED_SCORE)
            e = jnp.exp(scores - jnp.max(scores, axis=1, keepdims=True))
            probs = e * (1.0 / jnp.sum(e, axis=1, keepdims=True))
            probs_all[h, here, :] = probs
            outs.append(dot(probs.astype(jnp.bfloat16), v_all[...]))
        att_all[here, :] = jnp.where(first, outs[0], outs[1]).astype(jnp.bfloat16)
        return carry

    lax.fori_loop(0, n, forward, 0)

    core_copies = []
    for d in range(1, n):
        cot_copies[d - 1].wait_recv()
        block = cot_all.at[frames(source(d)), halfcols(core)]
        core_copies.append(remote(
            block, block, core_send.at[d], core_recv.at[d], {"tensor": 1 - core}))
        core_copies[-1].start()
    for copy in core_copies:
        copy.wait_recv()

    for c in range(2):
        gw_part[c] = dot(att_all[...], cot_all[:, c * half:(c + 1) * half], TN)
    gw_send[...] = gw_part[1 - side].astype(jnp.bfloat16)
    pair_copy = remote(gw_send, gw_recv, pair_send, pair_recv, {"dp": 1 - side})
    pair_copy.start()

    def project(i, carry):
        here = frames(i)
        dout_all[here, :] = dot(cot_all[here, :], w_ref[own, :], NT).astype(jnp.bfloat16)
        return carry

    lax.fori_loop(0, n, project, 0)
    dk_acc[...] = jnp.zeros_like(dk_acc)
    dv_acc[...] = jnp.zeros_like(dv_acc)

    def backward(i):
        here = frames(i)
        q = q_all[here, :]
        dout = dout_all[here, :]
        product = dout.astype(jnp.float32) * att_all[here, :].astype(jnp.float32)
        parts = []
        for h in range(2):
            delta = jnp.sum(product * masks[h], axis=1, keepdims=True)
            dout_h = dout * masks_low[h]
            probs = probs_all[h, here, :]
            grads = (probs * (dot(dout_h, v_all[...], NT) - delta) * scale).astype(jnp.bfloat16)
            parts.append(dot(grads, k_all[...]))
            dk_acc[...] += dot(q * masks_low[h], grads, TN)
            dv_acc[...] += dot(dout_h, probs.astype(jnp.bfloat16), TN)
        dq_all[here, :] = jnp.where(first, parts[0], parts[1]).astype(jnp.bfloat16)

    out_copies = []
    gz_copies = []
    gx_copies = []

    def pass_on(s, slot):
        block = gw_ref.at[pair(s), halfcols(side)]
        copy = remote(block, block, gx_send.at[slot], gx_recv.at[slot], {"dp": 1 - side})
        copy.start()
        gx_copies.append(copy)

    def send_out(t, src, dst, d):
        copy = remote(
            src.at[frames(peer(d)), :], dst.at[:, own],
            out_send.at[t, d], out_recv.at[t, d], {"seq": peer(d)})
        copy.start()
        out_copies.append(copy)

    for step in range(n):
        d = (step + 1) % n
        backward(peer(d))
        if d:
            send_out(0, dq_all, dq_ref, d)
        if step == 0:
            pair_copy.wait_recv()
            gw_ref[own, halfcols(side)] = (
                gw_part[side] + gw_recv[...].astype(jnp.float32)).astype(jnp.bfloat16)
            block = gw_ref.at[own, halfcols(side)]
            for e in range(1, n):
                copy = remote(block, block, gz_send.at[e], gz_recv.at[e], {"seq": peer(e)})
                copy.start()
                gz_copies.append(copy)
            pass_on(me, 0)

    dk_all[...] = jnp.transpose(dk_acc[...]).astype(jnp.bfloat16)
    for d in range(1, n):
        send_out(1, dk_all, dk_ref, d)
    dv_all[...] = jnp.transpose(dv_acc[...]).astype(jnp.bfloat16)
    for d in range(1, n):
        send_out(2, dv_all, dv_ref, d)
    dq_ref[:, own] = dq_all[frames(me), :]
    dk_ref[:, own] = dk_all[frames(me), :]
    dv_ref[:, own] = dv_all[frames(me), :]
    for d in range(1, n):
        gz_copies[d - 1].wait_recv()
        pass_on(source(d), d)
    for copy in gx_copies + out_copies:
        copy.wait_recv()
    for copy in in_copies + cot_copies + core_copies + [pair_copy] + gz_copies + gx_copies + out_copies:
        copy.wait_send()


def fused(n, queries, key_rows, value_rows, utterance, cotangent, out_weight):
    rows, width = queries.shape[1:]
    depth = cotangent.shape[2]
    total = n * rows
    wide = -(-rows // 128) * 128
    utts = jnp.broadcast_to(
        jnp.pad(utterance.astype(jnp.float32), ((0, 0), (0, wide - rows))), (8, wide))
    low, full = jnp.bfloat16, jnp.float32
    vmem = pl.BlockSpec(memory_space=pltpu.VMEM)
    dma = pltpu.SemaphoreType.DMA
    dq, dk, dv, gw = pl.pallas_call(
        functools.partial(fused_kernel, n),
        out_shape=[jax.ShapeDtypeStruct((rows, width), low)] * 3
        + [jax.ShapeDtypeStruct((width, depth), low)],
        in_specs=[vmem] * 6,
        out_specs=[vmem] * 4,
        scratch_shapes=[
            pltpu.VMEM((total, PAIR), low),
            pltpu.VMEM((total, PAIR), low),
            pltpu.VMEM((total, PAIR), low),
            pltpu.VMEM((n, 8, wide), full),
            pltpu.VMEM((total, depth), low),
            pltpu.VMEM((total, 128), full),
            pltpu.VMEM((8, total), full),
            pltpu.VMEM((2, total, total), full),
            pltpu.VMEM((total, PAIR), low),
            pltpu.VMEM((total, PAIR), low),
            pltpu.VMEM((total, PAIR), low),
            pltpu.VMEM((total, PAIR), low),
            pltpu.VMEM((total, PAIR), low),
            pltpu.VMEM((PAIR, total), full),
            pltpu.VMEM((PAIR, total), full),
            pltpu.VMEM((2, PAIR, depth // 2), full),
            pltpu.VMEM((PAIR, depth // 2), low),
            pltpu.VMEM((PAIR, depth // 2), low),
            dma((4, n)), dma((4, n)), dma((n,)), dma((n,)), dma((n,)), dma((n,)),
            dma((3, n)), dma((3, n)), dma, dma, dma((n,)), dma((n,)), dma((n,)), dma((n,)),
        ],
        compiler_params=pltpu.CompilerParams(
            collective_id=0, has_side_effects=True, vmem_limit_bytes=40 << 20),
    )(queries[0], key_rows[0], value_rows[0], utts, cotangent[0], out_weight)
    return dq[None], dk[None], dv[None], gw.astype(full)


def solution(mesh):
    n = mesh.shape["seq"]

    def body(*args):
        width, rows = args[0].shape[2], args[0].shape[1]
        fits = (
            width == n * PAIR and rows % 16 == 0 and n > 1
            and mesh.shape["dp"] == 2 and mesh.shape["tensor"] == 2
        )
        return fused(n, *args) if fits else local(*args)

    placed = (
        P(("groups", "dp"), "seq", "tensor"),
        P(("groups", "dp"), "seq", "tensor"),
        P(("groups", "dp"), "seq", "tensor"),
        P(("groups", "dp"), "seq"),
        P(("groups", "dp"), "seq", None),
        P("tensor", None),
    )
    return jax.shard_map(
        body,
        mesh=mesh,
        in_specs=placed,
        out_specs=(
            P(("groups", "dp"), "seq", "tensor"),
            P(("groups", "dp"), "seq", "tensor"),
            P(("groups", "dp"), "seq", "tensor"),
            P(("groups", "tensor"), None),
        ),
        check_vma=False,
    )
```

```python
import functools
import math

import jax
import jax.numpy as jnp
from jax import lax
from jax.experimental import pallas as pl
from jax.experimental.pallas import tpu as pltpu
from jax.sharding import PartitionSpec as P

HD = 64


MASKED_SCORE = -1e30


def heads_of(array):
    return array.reshape(array.shape[0], array.shape[1] // HD, HD)


def block_scores(query_block, key_block, query_utts, key_utts):
    scores = jnp.einsum(
        "qhd,khd->hqk", query_block, key_block, preferred_element_type=jnp.float32
    ) * HD ** (-0.5)
    same_utt = query_utts[:, None] == key_utts[None, :]
    return jnp.where(same_utt[None], scores, MASKED_SCORE)


def score_gradient(probs, dout_block, value_block, delta_rows):
    prob_grads = jnp.einsum(
        "qhd,khd->hqk", dout_block, value_block, preferred_element_type=jnp.float32
    )
    return (probs * (prob_grads - delta_rows[:, :, None]) * HD ** (-0.5)).astype(jnp.bfloat16)


def local(queries, key_rows, value_rows, utterance, cotangent, out_weight):
    own_queries = queries[0]
    frames_dev = own_queries.shape[0]
    width_dev = own_queries.shape[1]
    heads_dev = width_dev // HD
    query_heads = heads_of(own_queries)
    my_utts = utterance[0]
    utts_all = lax.all_gather(my_utts, "seq", axis=0, tiled=True)
    keys_all, values_all = (
        lax.all_gather(key_rows[0], "seq", axis=0, tiled=True),
        lax.all_gather(value_rows[0], "seq", axis=0, tiled=True),
    )
    frames_all = keys_all.shape[0]
    key_span = math.gcd(frames_all, 512)
    block_count = frames_all // key_span

    def key_block(block_index):
        offset = block_index * key_span
        key_block_rows = heads_of(lax.dynamic_slice_in_dim(keys_all, offset, key_span, 0))
        value_block_rows = heads_of(lax.dynamic_slice_in_dim(values_all, offset, key_span, 0))
        utt_block = lax.dynamic_slice_in_dim(utts_all, offset, key_span, 0)
        return (key_block_rows, value_block_rows, utt_block)

    def stats_step(block_index, carried):
        key_block_rows, value_block_rows, utt_block = key_block(block_index)
        running_max, running_sum = carried
        scores = block_scores(query_heads, key_block_rows, my_utts, utt_block)
        new_max = jnp.maximum(running_max, jnp.max(scores, axis=2))
        running_sum = running_sum * jnp.exp(running_max - new_max) + jnp.sum(
            jnp.exp(scores - new_max[:, :, None]), axis=2
        )
        return (new_max, running_sum)

    start_max = jnp.full((heads_dev, frames_dev), MASKED_SCORE, jnp.float32)
    start_sum = jnp.zeros((heads_dev, frames_dev), jnp.float32)
    running_max, running_sum = lax.fori_loop(0, block_count, stats_step, (start_max, start_sum))
    log_norm = running_max + jnp.log(running_sum)

    def output_step(block_index, carried):
        key_block_rows, value_block_rows, utt_block = key_block(block_index)
        scores = block_scores(query_heads, key_block_rows, my_utts, utt_block)
        probs_low = jnp.exp(scores - log_norm[:, :, None]).astype(jnp.bfloat16)
        return carried + jnp.einsum(
            "hqk,khd->hqd", probs_low, value_block_rows, preferred_element_type=jnp.float32
        )

    head_zeros = jnp.zeros((heads_dev, frames_dev, HD), jnp.float32)
    attended_acc = lax.fori_loop(0, block_count, output_step, head_zeros)
    attended = attended_acc.transpose(1, 0, 2).reshape(frames_dev, width_dev).astype(jnp.bfloat16)
    own_cot = cotangent[0]
    d_attended = lax.dot_general(
        own_cot, out_weight, (((1,), (1,)), ((), ())), preferred_element_type=jnp.float32
    ).astype(jnp.bfloat16)
    weight_term = lax.dot_general(
        attended, own_cot, (((0,), (0,)), ((), ())), preferred_element_type=jnp.float32
    )
    grad_weight = lax.psum(weight_term, ("seq", "dp"))
    dout_heads = heads_of(d_attended)
    row_delta = jnp.einsum(
        "qhd,qhd->hq", dout_heads.astype(jnp.float32), heads_of(attended).astype(jnp.float32)
    )

    def joint_step(block_index, carried):
        key_block_rows, value_block_rows, utt_block = key_block(block_index)
        query_acc_now, buffer = carried
        scores = block_scores(query_heads, key_block_rows, my_utts, utt_block)
        probs = jnp.exp(scores - log_norm[:, :, None])
        score_grads = score_gradient(probs, dout_heads, value_block_rows, row_delta)
        query_acc_now = query_acc_now + jnp.einsum(
            "hqk,khd->hqd", score_grads, key_block_rows, preferred_element_type=jnp.float32
        )
        key_part = jnp.einsum(
            "hqk,qhd->khd", score_grads, query_heads, preferred_element_type=jnp.float32
        )
        value_part = jnp.einsum(
            "hqk,qhd->khd",
            probs.astype(jnp.bfloat16),
            dout_heads,
            preferred_element_type=jnp.float32,
        )
        joined = jnp.concatenate(
            [key_part.reshape(key_span, width_dev), value_part.reshape(key_span, width_dev)], axis=1
        )
        buffer = lax.dynamic_update_slice_in_dim(buffer, joined, block_index * key_span, 0)
        return (query_acc_now, buffer)

    term_zeros = jnp.zeros((frames_all, 2 * width_dev), jnp.float32)
    query_acc, terms_all = lax.fori_loop(0, block_count, joint_step, (head_zeros, term_zeros))
    summed = lax.psum_scatter(terms_all, "seq", scatter_dimension=0, tiled=True)
    grad_key = summed[:, :width_dev].astype(jnp.bfloat16)
    grad_value = summed[:, width_dev:].astype(jnp.bfloat16)
    grad_query = query_acc.transpose(1, 0, 2).reshape(frames_dev, width_dev).astype(jnp.bfloat16)
    return (grad_query[None], grad_key[None], grad_value[None], grad_weight)


PAIR = 2 * HD
NT = (((1,), (1,)), ((), ()))
TN = (((0,), (0,)), ((), ()))
MESH = pl.DeviceIdType.MESH
CUTS = 2


def dot(a, b, dims=(((1,), (0,)), ((), ()))):
    return lax.dot_general(a, b, dims, preferred_element_type=jnp.float32)


def fused_kernel(
    n, q_ref, k_ref, v_ref, utt_ref, cot_ref, w_ref,
    dq_ref, dk_ref, dv_ref, gw_ref,
    q_all, k_all, v_all, utt_pad, utt_all, cot_all, w_own, utt_col, utt_row, probs_all, att_all,
    dq_all, dk_all, dv_all, dk_acc, dv_acc, gw_part, gw_send, gw_recv,
    local_sem, in_send, in_recv, cot_send, cot_recv, core_send, core_recv,
    out_send, out_recv, pair_send, pair_recv, gz_send, gz_recv, gx_send, gx_recv,
):
    me = lax.axis_index("seq")
    core = lax.axis_index("tensor")
    side = lax.axis_index("dp")
    rows = q_ref.shape[0]
    scale = HD ** -0.5

    def peer(d):
        return lax.rem(me + d, n)

    def frames(s):
        return pl.ds(pl.multiple_of(s * rows, rows), rows)

    def pair(s):
        return pl.ds(pl.multiple_of(s * PAIR, PAIR), PAIR)

    def slab(base, extent, who, cut):
        size = extent // (2 * CUTS)
        return pl.ds(pl.multiple_of(base + who * (extent // 2) + cut * size, size), size)

    def remote(src, dst, ssem, rsem, target):
        return pltpu.make_async_remote_copy(
            src_ref=src, dst_ref=dst, send_sem=ssem, recv_sem=rsem,
            device_id=target, device_id_type=MESH,
        )

    barrier = pltpu.get_barrier_semaphore()
    for d in range(1, n):
        pl.semaphore_signal(barrier, inc=1, device_id={"seq": peer(d)}, device_id_type=MESH)
    pl.semaphore_signal(barrier, inc=1, device_id={"tensor": 1 - core}, device_id_type=MESH)
    pl.semaphore_signal(barrier, inc=1, device_id={"dp": 1 - side}, device_id_type=MESH)

    own = pair(me)
    local_copies = [
        pltpu.make_async_copy(src, dst, local_sem.at[i])
        for i, (src, dst) in enumerate((
            (q_ref.at[:, own], q_all.at[frames(me), :]),
            (k_ref.at[:, own], k_all.at[frames(me), :]),
            (v_ref.at[:, own], v_all.at[frames(me), :]),
            (cot_ref, cot_all.at[frames(me), :]),
            (w_ref.at[own, :], w_own),
        ))
    ]
    for copy in local_copies:
        copy.start()
    utt_pad[...] = jnp.zeros_like(utt_pad)
    utt_pad[0:1, 0:rows] = utt_ref[...].astype(jnp.float32)
    utt_all[me] = utt_pad[...]

    order = [jnp.int32(0)] * (n - 1)
    count = jnp.int32(0)
    for dist in range(1, n):
        for s in (me - dist, me + dist):
            valid = jnp.logical_and(s >= 0, s < n)
            for k in range(n - 1):
                order[k] = jnp.where(jnp.logical_and(valid, count == k), s, order[k])
            count = count + valid.astype(jnp.int32)

    def onward(src, dst, s, cut, ssem, rsem, act):
        @pl.when(jnp.logical_and(s <= me, me < n - 1))
        def _():
            act(remote(src, dst, ssem.at[0, s, cut], rsem.at[s, cut], {"seq": lax.rem(me + 1, n)}))

        @pl.when(jnp.logical_and(s >= me, me > 0))
        def _():
            act(remote(src, dst, ssem.at[1, s, cut], rsem.at[s, cut], {"seq": lax.rem(me + n - 1, n)}))

    start = lambda copy: copy.start()
    wait_send = lambda copy: copy.wait_send()

    pl.semaphore_wait(barrier, n + 1)
    in_copies = []
    for d in range(1, n):
        to = {"seq": peer(d)}
        cols = pair(peer(d))
        in_copies.append(remote(utt_pad, utt_all.at[me], in_send.at[3, d], in_recv.at[3, d], to))
        for t, (src, dst) in enumerate(((k_ref, k_all), (v_ref, v_all), (q_ref, q_all))):
            in_copies.append(remote(
                src.at[:, cols], dst.at[frames(me), :], in_send.at[t, d], in_recv.at[t, d], to))
    for copy in in_copies:
        copy.start()

    def cot_block(s, cut):
        return cot_all.at[slab(s * rows, rows, core, cut), :]

    for cut in range(CUTS):
        onward(cot_ref.at[slab(0, rows, core, cut), :], cot_block(me, cut), me, cut,
               cot_send, cot_recv, start)
    for copy in local_copies:
        copy.wait()
    for copy in in_copies:
        copy.wait_recv()

    for s in range(n):
        wide = jnp.broadcast_to(utt_all[s, 0:1, :], (128, utt_all.shape[2]))
        utt_col[s * rows:(s + 1) * rows, :] = jnp.transpose(wide)[:rows, :]
    utt_row[...] = jnp.transpose(utt_col[...])[0:8, :]

    lane = lax.broadcasted_iota(jnp.int32, (rows, PAIR), 1)
    first = lane < HD
    masks = [first.astype(jnp.float32), (lane >= HD).astype(jnp.float32)]
    masks_low = [m.astype(jnp.bfloat16) for m in masks]

    def forward(i):
        here = frames(i)
        q = q_all[here, :]
        same = utt_col[here, 0:1] == utt_row[0:1, :]
        outs = []
        for h in range(2):
            scores = dot(q * masks_low[h], k_all[...], NT) * scale
            scores = jnp.where(same, scores, MASKED_SCORE)
            e = jnp.exp(scores - jnp.max(scores, axis=1, keepdims=True))
            probs = e * (1.0 / jnp.sum(e, axis=1, keepdims=True))
            probs_all[h, here, :] = probs
            outs.append(dot(probs.astype(jnp.bfloat16), v_all[...]))
        att_all[here, :] = jnp.where(first, outs[0], outs[1]).astype(jnp.bfloat16)

    def forward_step(i, carry):
        forward(i)
        return carry

    core_copies = []

    def take_cot(k):
        s = order[k]
        for cut in range(CUTS):
            block = cot_block(s, cut)
            copy = remote(
                block, block, core_send.at[k, cut], core_recv.at[k, cut], {"tensor": 1 - core})
            remote(block, block, core_send.at[k, cut], cot_recv.at[s, cut],
                   {"tensor": 1 - core}).wait_recv()
            onward(block, block, s, cut, cot_send, cot_recv, start)
            copy.start()
            core_copies.append(copy)

    gw_part[...] = jnp.zeros_like(gw_part)
    dk_acc[...] = jnp.zeros_like(dk_acc)
    dv_acc[...] = jnp.zeros_like(dv_acc)
    lax.fori_loop(0, n // 2, forward_step, 0)
    take_cot(0)
    lax.fori_loop(n // 2, n, forward_step, 0)

    def slab_half(who):
        return pl.ds(pl.multiple_of(who * HD, HD), HD)

    def weigh(i):
        here = frames(i)
        gw_part[...] += dot(att_all[here, :], cot_all[here, :], TN)

    def backward(i):
        here = frames(i)
        q = q_all[here, :]
        dout = dot(cot_all[here, :], w_own[...], NT).astype(jnp.bfloat16)
        product = dout.astype(jnp.float32) * att_all[here, :].astype(jnp.float32)
        parts = []
        for h in range(2):
            delta = jnp.sum(product * masks[h], axis=1, keepdims=True)
            dout_h = dout * masks_low[h]
            probs = probs_all[h, here, :]
            grads = (probs * (dot(dout_h, v_all[...], NT) - delta) * scale).astype(jnp.bfloat16)
            parts.append(dot(grads, k_all[...]))
            dk_acc[...] += dot(q * masks_low[h], grads, TN)
            dv_acc[...] += dot(dout_h, probs.astype(jnp.bfloat16), TN)
        dq_all[here, :] = jnp.where(first, parts[0], parts[1]).astype(jnp.bfloat16)

    out_copies = []

    def send_out(t, src, dst, to):
        d = lax.rem(to - me + n, n)
        copy = remote(
            src.at[frames(to), :], dst.at[:, own],
            out_send.at[t, d], out_recv.at[t, d], {"seq": to})
        copy.start()
        out_copies.append(copy)

    weigh(me)
    backward(me)
    for k in range(n - 1):
        if k:
            take_cot(k)
        for copy in core_copies[k * CUTS:(k + 1) * CUTS]:
            copy.wait_recv()
        weigh(order[k])
        if k == n - 2:
            gw_send[...] = gw_part[slab_half(1 - side), :].astype(jnp.bfloat16)
            pair_copy = remote(gw_send, gw_recv, pair_send, pair_recv, {"dp": 1 - side})
            pair_copy.start()
        backward(order[k])
        send_out(0, dq_all, dq_ref, order[k])

    dk_all[...] = jnp.transpose(dk_acc[...]).astype(jnp.bfloat16)
    dv_all[...] = jnp.transpose(dv_acc[...]).astype(jnp.bfloat16)

    gx_copies = []

    def gw_block(s, cut):
        return gw_ref.at[slab(s * PAIR, PAIR, side, cut), :]

    def pass_on(s, slot, cut):
        block = gw_block(s, cut)
        copy = remote(
            block, block, gx_send.at[slot, cut], gx_recv.at[slot, cut], {"dp": 1 - side})
        copy.start()
        gx_copies.append(copy)

    pair_copy.wait_recv()
    gw_ref[pl.ds(pl.multiple_of(me * PAIR + side * HD, HD), HD), :] = (
        gw_part[slab_half(side), :] + gw_recv[...].astype(jnp.float32)).astype(jnp.bfloat16)
    for cut in range(CUTS):
        onward(gw_block(me, cut), gw_block(me, cut), me, cut, gz_send, gz_recv, start)
    for cut in range(CUTS):
        pass_on(me, n - 1, cut)
    for t, (src, dst) in ((1, (dk_all, dk_ref)), (2, (dv_all, dv_ref))):
        for d in range(1, n):
            send_out(t, src, dst, peer(d))
    dq_ref[:, own] = dq_all[frames(me), :]
    dk_ref[:, own] = dk_all[frames(me), :]
    dv_ref[:, own] = dv_all[frames(me), :]
    for k in range(n - 1):
        s = order[k]
        for cut in range(CUTS):
            block = gw_block(s, cut)
            remote(block, block, gx_send.at[k, cut], gz_recv.at[s, cut],
                   {"dp": 1 - side}).wait_recv()
            onward(block, block, s, cut, gz_send, gz_recv, start)
            pass_on(s, k, cut)
    for copy in gx_copies + out_copies:
        copy.wait_recv()
    for s in [me] + order:
        for cut in range(CUTS):
            block, done = cot_block(s, cut), gw_block(s, cut)
            onward(block, block, s, cut, cot_send, cot_recv, wait_send)
            onward(done, done, s, cut, gz_send, gz_recv, wait_send)
    for copy in in_copies + core_copies + [pair_copy] + gx_copies + out_copies:
        copy.wait_send()


def fused(n, queries, key_rows, value_rows, utterance, cotangent, out_weight):
    rows, width = queries.shape[1:]
    depth = cotangent.shape[2]
    total = n * rows
    wide = -(-rows // 128) * 128
    low, full = jnp.bfloat16, jnp.float32
    vmem = pl.BlockSpec(memory_space=pltpu.VMEM)
    hbm = pl.BlockSpec(memory_space=pltpu.HBM)
    dma = pltpu.SemaphoreType.DMA
    dq, dk, dv, gw = pl.pallas_call(
        functools.partial(fused_kernel, n),
        out_shape=[jax.ShapeDtypeStruct((rows, width), low)] * 3
        + [jax.ShapeDtypeStruct((width, depth), low)],
        in_specs=[hbm, hbm, hbm, vmem, hbm, hbm],
        out_specs=[vmem] * 4,
        scratch_shapes=[
            pltpu.VMEM((total, PAIR), low),
            pltpu.VMEM((total, PAIR), low),
            pltpu.VMEM((total, PAIR), low),
            pltpu.VMEM((8, wide), full),
            pltpu.VMEM((n, 8, wide), full),
            pltpu.VMEM((total, depth), low),
            pltpu.VMEM((PAIR, depth), low),
            pltpu.VMEM((total, 128), full),
            pltpu.VMEM((8, total), full),
            pltpu.VMEM((2, total, total), full),
            pltpu.VMEM((total, PAIR), low),
            pltpu.VMEM((total, PAIR), low),
            pltpu.VMEM((total, PAIR), low),
            pltpu.VMEM((total, PAIR), low),
            pltpu.VMEM((PAIR, total), full),
            pltpu.VMEM((PAIR, total), full),
            pltpu.VMEM((PAIR, depth), full),
            pltpu.VMEM((HD, depth), low),
            pltpu.VMEM((HD, depth), low),
            dma((5,)), dma((4, n)), dma((4, n)), dma((2, n, CUTS)), dma((n, CUTS)),
            dma((n, CUTS)), dma((n, CUTS)), dma((3, n)), dma((3, n)), dma, dma,
            dma((2, n, CUTS)), dma((n, CUTS)), dma((n, CUTS)), dma((n, CUTS)),
        ],
        compiler_params=pltpu.CompilerParams(
            collective_id=0, has_side_effects=True, vmem_limit_bytes=60 << 20),
    )(queries[0], key_rows[0], value_rows[0], utterance, cotangent[0], out_weight)
    return dq[None], dk[None], dv[None], gw.astype(full)


def solution(mesh):
    n = mesh.shape["seq"]

    def body(*args):
        width, rows = args[0].shape[2], args[0].shape[1]
        fits = (
            width == n * PAIR and rows % (32 * CUTS) == 0 and n > 1
            and mesh.shape["dp"] == 2 and mesh.shape["tensor"] == 2
        )
        return fused(n, *args) if fits else local(*args)

    placed = (
        P(("groups", "dp"), "seq", "tensor"),
        P(("groups", "dp"), "seq", "tensor"),
        P(("groups", "dp"), "seq", "tensor"),
        P(("groups", "dp"), "seq"),
        P(("groups", "dp"), "seq", None),
        P("tensor", None),
    )
    return jax.shard_map(
        body,
        mesh=mesh,
        in_specs=placed,
        out_specs=(
            P(("groups", "dp"), "seq", "tensor"),
            P(("groups", "dp"), "seq", "tensor"),
            P(("groups", "dp"), "seq", "tensor"),
            P(("groups", "tensor"), None),
        ),
        check_vma=False,
    )
```

```python
import functools
import math

import jax
import jax.numpy as jnp
from jax import lax
from jax.experimental import pallas as pl
from jax.experimental.pallas import tpu as pltpu
from jax.sharding import PartitionSpec as P

HD = 64


MASKED_SCORE = -1e30


def heads_of(array):
    return array.reshape(array.shape[0], array.shape[1] // HD, HD)


def block_scores(query_block, key_block, query_utts, key_utts):
    scores = jnp.einsum(
        "qhd,khd->hqk", query_block, key_block, preferred_element_type=jnp.float32
    ) * HD ** (-0.5)
    same_utt = query_utts[:, None] == key_utts[None, :]
    return jnp.where(same_utt[None], scores, MASKED_SCORE)


def score_gradient(probs, dout_block, value_block, delta_rows):
    prob_grads = jnp.einsum(
        "qhd,khd->hqk", dout_block, value_block, preferred_element_type=jnp.float32
    )
    return (probs * (prob_grads - delta_rows[:, :, None]) * HD ** (-0.5)).astype(jnp.bfloat16)


def local(queries, key_rows, value_rows, utterance, cotangent, out_weight):
    own_queries = queries[0]
    frames_dev = own_queries.shape[0]
    width_dev = own_queries.shape[1]
    heads_dev = width_dev // HD
    query_heads = heads_of(own_queries)
    my_utts = utterance[0]
    utts_all = lax.all_gather(my_utts, "seq", axis=0, tiled=True)
    keys_all, values_all = (
        lax.all_gather(key_rows[0], "seq", axis=0, tiled=True),
        lax.all_gather(value_rows[0], "seq", axis=0, tiled=True),
    )
    frames_all = keys_all.shape[0]
    key_span = math.gcd(frames_all, 512)
    block_count = frames_all // key_span

    def key_block(block_index):
        offset = block_index * key_span
        key_block_rows = heads_of(lax.dynamic_slice_in_dim(keys_all, offset, key_span, 0))
        value_block_rows = heads_of(lax.dynamic_slice_in_dim(values_all, offset, key_span, 0))
        utt_block = lax.dynamic_slice_in_dim(utts_all, offset, key_span, 0)
        return (key_block_rows, value_block_rows, utt_block)

    def stats_step(block_index, carried):
        key_block_rows, value_block_rows, utt_block = key_block(block_index)
        running_max, running_sum = carried
        scores = block_scores(query_heads, key_block_rows, my_utts, utt_block)
        new_max = jnp.maximum(running_max, jnp.max(scores, axis=2))
        running_sum = running_sum * jnp.exp(running_max - new_max) + jnp.sum(
            jnp.exp(scores - new_max[:, :, None]), axis=2
        )
        return (new_max, running_sum)

    start_max = jnp.full((heads_dev, frames_dev), MASKED_SCORE, jnp.float32)
    start_sum = jnp.zeros((heads_dev, frames_dev), jnp.float32)
    running_max, running_sum = lax.fori_loop(0, block_count, stats_step, (start_max, start_sum))
    log_norm = running_max + jnp.log(running_sum)

    def output_step(block_index, carried):
        key_block_rows, value_block_rows, utt_block = key_block(block_index)
        scores = block_scores(query_heads, key_block_rows, my_utts, utt_block)
        probs_low = jnp.exp(scores - log_norm[:, :, None]).astype(jnp.bfloat16)
        return carried + jnp.einsum(
            "hqk,khd->hqd", probs_low, value_block_rows, preferred_element_type=jnp.float32
        )

    head_zeros = jnp.zeros((heads_dev, frames_dev, HD), jnp.float32)
    attended_acc = lax.fori_loop(0, block_count, output_step, head_zeros)
    attended = attended_acc.transpose(1, 0, 2).reshape(frames_dev, width_dev).astype(jnp.bfloat16)
    own_cot = cotangent[0]
    d_attended = lax.dot_general(
        own_cot, out_weight, (((1,), (1,)), ((), ())), preferred_element_type=jnp.float32
    ).astype(jnp.bfloat16)
    weight_term = lax.dot_general(
        attended, own_cot, (((0,), (0,)), ((), ())), preferred_element_type=jnp.float32
    )
    grad_weight = lax.psum(weight_term, ("seq", "dp"))
    dout_heads = heads_of(d_attended)
    row_delta = jnp.einsum(
        "qhd,qhd->hq", dout_heads.astype(jnp.float32), heads_of(attended).astype(jnp.float32)
    )

    def joint_step(block_index, carried):
        key_block_rows, value_block_rows, utt_block = key_block(block_index)
        query_acc_now, buffer = carried
        scores = block_scores(query_heads, key_block_rows, my_utts, utt_block)
        probs = jnp.exp(scores - log_norm[:, :, None])
        score_grads = score_gradient(probs, dout_heads, value_block_rows, row_delta)
        query_acc_now = query_acc_now + jnp.einsum(
            "hqk,khd->hqd", score_grads, key_block_rows, preferred_element_type=jnp.float32
        )
        key_part = jnp.einsum(
            "hqk,qhd->khd", score_grads, query_heads, preferred_element_type=jnp.float32
        )
        value_part = jnp.einsum(
            "hqk,qhd->khd",
            probs.astype(jnp.bfloat16),
            dout_heads,
            preferred_element_type=jnp.float32,
        )
        joined = jnp.concatenate(
            [key_part.reshape(key_span, width_dev), value_part.reshape(key_span, width_dev)], axis=1
        )
        buffer = lax.dynamic_update_slice_in_dim(buffer, joined, block_index * key_span, 0)
        return (query_acc_now, buffer)

    term_zeros = jnp.zeros((frames_all, 2 * width_dev), jnp.float32)
    query_acc, terms_all = lax.fori_loop(0, block_count, joint_step, (head_zeros, term_zeros))
    summed = lax.psum_scatter(terms_all, "seq", scatter_dimension=0, tiled=True)
    grad_key = summed[:, :width_dev].astype(jnp.bfloat16)
    grad_value = summed[:, width_dev:].astype(jnp.bfloat16)
    grad_query = query_acc.transpose(1, 0, 2).reshape(frames_dev, width_dev).astype(jnp.bfloat16)
    return (grad_query[None], grad_key[None], grad_value[None], grad_weight)


PAIR = 2 * HD
NT = (((1,), (1,)), ((), ()))
TN = (((0,), (0,)), ((), ()))
MESH = pl.DeviceIdType.MESH
CUTS = 2


def dot(a, b, dims=(((1,), (0,)), ((), ()))):
    return lax.dot_general(a, b, dims, preferred_element_type=jnp.float32)


def fused_kernel(
    n, q_ref, k_ref, v_ref, utt_ref, cot_ref, w_ref,
    dq_ref, dk_ref, dv_ref, gw_ref,
    q_all, k_all, v_all, utt_pad, utt_all, cot_all, w_own, utt_col, utt_row, probs_all, att_all,
    dq_all, dk_all, dv_all, dk_acc, dv_acc, gw_part, gw_send, gw_recv,
    local_sem, in_send, in_recv, cot_send, cot_recv, core_send, core_recv,
    out_send, out_recv, pair_send, pair_recv, gz_send, gz_recv, gx_send, gx_recv,
):
    me = lax.axis_index("seq")
    core = lax.axis_index("tensor")
    side = lax.axis_index("dp")
    rows = q_ref.shape[0]
    scale = HD ** -0.5

    def peer(d):
        return lax.rem(me + d, n)

    def frames(s):
        return pl.ds(pl.multiple_of(s * rows, rows), rows)

    def pair(s):
        return pl.ds(pl.multiple_of(s * PAIR, PAIR), PAIR)

    def slab(base, extent, who, cut):
        size = extent // (2 * CUTS)
        return pl.ds(pl.multiple_of(base + who * (extent // 2) + cut * size, size), size)

    def remote(src, dst, ssem, rsem, target):
        return pltpu.make_async_remote_copy(
            src_ref=src, dst_ref=dst, send_sem=ssem, recv_sem=rsem,
            device_id=target, device_id_type=MESH,
        )

    barrier = pltpu.get_barrier_semaphore()
    for d in range(1, n):
        pl.semaphore_signal(barrier, inc=1, device_id={"seq": peer(d)}, device_id_type=MESH)
    pl.semaphore_signal(barrier, inc=1, device_id={"tensor": 1 - core}, device_id_type=MESH)
    pl.semaphore_signal(barrier, inc=1, device_id={"dp": 1 - side}, device_id_type=MESH)

    own = pair(me)
    local_copies = [
        pltpu.make_async_copy(src, dst, local_sem.at[i])
        for i, (src, dst) in enumerate((
            (q_ref.at[:, own], q_all.at[frames(me), :]),
            (k_ref.at[:, own], k_all.at[frames(me), :]),
            (v_ref.at[:, own], v_all.at[frames(me), :]),
            (cot_ref, cot_all.at[frames(me), :]),
            (w_ref.at[own, :], w_own),
        ))
    ]
    for copy in local_copies:
        copy.start()
    utt_pad[...] = jnp.zeros_like(utt_pad)
    utt_pad[0:1, 0:rows] = utt_ref[...].astype(jnp.float32)
    utt_all[me] = utt_pad[...]

    order = [jnp.int32(0)] * (n - 1)
    count = jnp.int32(0)
    for dist in range(1, n):
        for s in (me - dist, me + dist):
            valid = jnp.logical_and(s >= 0, s < n)
            for k in range(n - 1):
                order[k] = jnp.where(jnp.logical_and(valid, count == k), s, order[k])
            count = count + valid.astype(jnp.int32)

    def onward(src, dst, s, cut, ssem, rsem, act):
        @pl.when(jnp.logical_and(s <= me, me < n - 1))
        def _():
            act(remote(src, dst, ssem.at[0, s, cut], rsem.at[s, cut], {"seq": lax.rem(me + 1, n)}))

        @pl.when(jnp.logical_and(s >= me, me > 0))
        def _():
            act(remote(src, dst, ssem.at[1, s, cut], rsem.at[s, cut], {"seq": lax.rem(me + n - 1, n)}))

    start = lambda copy: copy.start()
    wait_send = lambda copy: copy.wait_send()

    pl.semaphore_wait(barrier, n + 1)
    in_copies = []
    for d in range(1, n):
        to = {"seq": peer(d)}
        cols = pair(peer(d))
        in_copies.append(remote(utt_pad, utt_all.at[me], in_send.at[3, d], in_recv.at[3, d], to))
        for t, (src, dst) in enumerate(((k_ref, k_all), (v_ref, v_all), (q_ref, q_all))):
            in_copies.append(remote(
                src.at[:, cols], dst.at[frames(me), :], in_send.at[t, d], in_recv.at[t, d], to))

    def cot_block(s, cut):
        return cot_all.at[slab(s * rows, rows, core, cut), :]

    for cut in range(CUTS):
        onward(cot_ref.at[slab(0, rows, core, cut), :], cot_block(me, cut), me, cut,
               cot_send, cot_recv, start)
    for copy in in_copies:
        copy.start()
    for copy in local_copies:
        copy.wait()
    core_copies = []

    def take_cot(k):
        s = order[k]
        for cut in range(CUTS):
            block = cot_block(s, cut)
            copy = remote(
                block, block, core_send.at[k, cut], core_recv.at[k, cut], {"tensor": 1 - core})
            remote(block, block, core_send.at[k, cut], cot_recv.at[s, cut],
                   {"tensor": 1 - core}).wait_recv()
            onward(block, block, s, cut, cot_send, cot_recv, start)
            copy.start()
            core_copies.append(copy)

    take_cot(0)
    take_cot(1)
    for copy in in_copies:
        copy.wait_recv()

    for s in range(n):
        wide = jnp.broadcast_to(utt_all[s, 0:1, :], (128, utt_all.shape[2]))
        utt_col[s * rows:(s + 1) * rows, :] = jnp.transpose(wide)[:rows, :]
    utt_row[...] = jnp.transpose(utt_col[...])[0:8, :]

    lane = lax.broadcasted_iota(jnp.int32, (rows, PAIR), 1)
    first = lane < HD
    masks = [first.astype(jnp.float32), (lane >= HD).astype(jnp.float32)]
    masks_low = [m.astype(jnp.bfloat16) for m in masks]

    def forward(i):
        here = frames(i)
        q = q_all[here, :]
        same = utt_col[here, 0:1] == utt_row[0:1, :]
        outs = []
        for h in range(2):
            scores = dot(q * masks_low[h], k_all[...], NT) * scale
            scores = jnp.where(same, scores, MASKED_SCORE)
            e = jnp.exp(scores - jnp.max(scores, axis=1, keepdims=True))
            probs = e * (1.0 / jnp.sum(e, axis=1, keepdims=True))
            probs_all[h, here, :] = probs
            outs.append(dot(probs.astype(jnp.bfloat16), v_all[...]))
        att_all[here, :] = jnp.where(first, outs[0], outs[1]).astype(jnp.bfloat16)

    def forward_step(i, carry):
        forward(i)
        return carry

    gw_part[...] = jnp.zeros_like(gw_part)
    dk_acc[...] = jnp.zeros_like(dk_acc)
    dv_acc[...] = jnp.zeros_like(dv_acc)
    lax.fori_loop(0, n // 2, forward_step, 0)
    lax.fori_loop(n // 2, n, forward_step, 0)

    def slab_half(who):
        return pl.ds(pl.multiple_of(who * HD, HD), HD)

    def weigh(i):
        here = frames(i)
        gw_part[...] += dot(att_all[here, :], cot_all[here, :], TN)

    def backward(i):
        here = frames(i)
        q = q_all[here, :]
        dout = dot(cot_all[here, :], w_own[...], NT).astype(jnp.bfloat16)
        product = dout.astype(jnp.float32) * att_all[here, :].astype(jnp.float32)
        parts = []
        for h in range(2):
            delta = jnp.sum(product * masks[h], axis=1, keepdims=True)
            dout_h = dout * masks_low[h]
            probs = probs_all[h, here, :]
            grads = (probs * (dot(dout_h, v_all[...], NT) - delta) * scale).astype(jnp.bfloat16)
            parts.append(dot(grads, k_all[...]))
            dk_acc[...] += dot(q * masks_low[h], grads, TN)
            dv_acc[...] += dot(dout_h, probs.astype(jnp.bfloat16), TN)
        dq_all[here, :] = jnp.where(first, parts[0], parts[1]).astype(jnp.bfloat16)

    out_copies = []

    def send_out(t, src, dst, to):
        d = lax.rem(to - me + n, n)
        copy = remote(
            src.at[frames(to), :], dst.at[:, own],
            out_send.at[t, d], out_recv.at[t, d], {"seq": to})
        copy.start()
        out_copies.append(copy)

    weigh(me)
    backward(me)
    for k in range(n - 1):
        if k >= 2:
            take_cot(k)
        for copy in core_copies[k * CUTS:(k + 1) * CUTS]:
            copy.wait_recv()
        weigh(order[k])
        if k == n - 2:
            gw_send[...] = gw_part[slab_half(1 - side), :].astype(jnp.bfloat16)
            pair_copy = remote(gw_send, gw_recv, pair_send, pair_recv, {"dp": 1 - side})
            pair_copy.start()
        backward(order[k])
        send_out(0, dq_all, dq_ref, order[k])

    dk_all[...] = jnp.transpose(dk_acc[...]).astype(jnp.bfloat16)
    dv_all[...] = jnp.transpose(dv_acc[...]).astype(jnp.bfloat16)

    gx_copies = []

    def gw_block(s, cut):
        return gw_ref.at[slab(s * PAIR, PAIR, side, cut), :]

    def pass_on(s, slot, cut):
        block = gw_block(s, cut)
        copy = remote(
            block, block, gx_send.at[slot, cut], gx_recv.at[slot, cut], {"dp": 1 - side})
        copy.start()
        gx_copies.append(copy)

    pair_copy.wait_recv()
    gw_ref[pl.ds(pl.multiple_of(me * PAIR + side * HD, HD), HD), :] = (
        gw_part[slab_half(side), :] + gw_recv[...].astype(jnp.float32)).astype(jnp.bfloat16)
    for cut in range(CUTS):
        onward(gw_block(me, cut), gw_block(me, cut), me, cut, gz_send, gz_recv, start)
    for cut in range(CUTS):
        pass_on(me, n - 1, cut)
    for t, (src, dst) in ((1, (dk_all, dk_ref)), (2, (dv_all, dv_ref))):
        for d in range(1, n):
            send_out(t, src, dst, peer(d))
    dq_ref[:, own] = dq_all[frames(me), :]
    dk_ref[:, own] = dk_all[frames(me), :]
    dv_ref[:, own] = dv_all[frames(me), :]
    for k in range(n - 1):
        s = order[k]
        for cut in range(CUTS):
            block = gw_block(s, cut)
            remote(block, block, gx_send.at[k, cut], gz_recv.at[s, cut],
                   {"dp": 1 - side}).wait_recv()
            onward(block, block, s, cut, gz_send, gz_recv, start)
            pass_on(s, k, cut)
    for copy in gx_copies + out_copies:
        copy.wait_recv()
    for s in [me] + order:
        for cut in range(CUTS):
            block, done = cot_block(s, cut), gw_block(s, cut)
            onward(block, block, s, cut, cot_send, cot_recv, wait_send)
            onward(done, done, s, cut, gz_send, gz_recv, wait_send)
    for copy in in_copies + core_copies + [pair_copy] + gx_copies + out_copies:
        copy.wait_send()


def fused(n, queries, key_rows, value_rows, utterance, cotangent, out_weight):
    rows, width = queries.shape[1:]
    depth = cotangent.shape[2]
    total = n * rows
    wide = -(-rows // 128) * 128
    low, full = jnp.bfloat16, jnp.float32
    vmem = pl.BlockSpec(memory_space=pltpu.VMEM)
    hbm = pl.BlockSpec(memory_space=pltpu.HBM)
    dma = pltpu.SemaphoreType.DMA
    dq, dk, dv, gw = pl.pallas_call(
        functools.partial(fused_kernel, n),
        out_shape=[jax.ShapeDtypeStruct((rows, width), low)] * 3
        + [jax.ShapeDtypeStruct((width, depth), low)],
        in_specs=[hbm, hbm, hbm, vmem, hbm, hbm],
        out_specs=[vmem] * 4,
        scratch_shapes=[
            pltpu.VMEM((total, PAIR), low),
            pltpu.VMEM((total, PAIR), low),
            pltpu.VMEM((total, PAIR), low),
            pltpu.VMEM((8, wide), full),
            pltpu.VMEM((n, 8, wide), full),
            pltpu.VMEM((total, depth), low),
            pltpu.VMEM((PAIR, depth), low),
            pltpu.VMEM((total, 128), full),
            pltpu.VMEM((8, total), full),
            pltpu.VMEM((2, total, total), full),
            pltpu.VMEM((total, PAIR), low),
            pltpu.VMEM((total, PAIR), low),
            pltpu.VMEM((total, PAIR), low),
            pltpu.VMEM((total, PAIR), low),
            pltpu.VMEM((PAIR, total), full),
            pltpu.VMEM((PAIR, total), full),
            pltpu.VMEM((PAIR, depth), full),
            pltpu.VMEM((HD, depth), low),
            pltpu.VMEM((HD, depth), low),
            dma((5,)), dma((4, n)), dma((4, n)), dma((2, n, CUTS)), dma((n, CUTS)),
            dma((n, CUTS)), dma((n, CUTS)), dma((3, n)), dma((3, n)), dma, dma,
            dma((2, n, CUTS)), dma((n, CUTS)), dma((n, CUTS)), dma((n, CUTS)),
        ],
        compiler_params=pltpu.CompilerParams(
            collective_id=0, has_side_effects=True, vmem_limit_bytes=60 << 20),
    )(queries[0], key_rows[0], value_rows[0], utterance, cotangent[0], out_weight)
    return dq[None], dk[None], dv[None], gw.astype(full)


def solution(mesh):
    n = mesh.shape["seq"]

    def body(*args):
        width, rows = args[0].shape[2], args[0].shape[1]
        fits = (
            width == n * PAIR and rows % (32 * CUTS) == 0 and n > 1
            and mesh.shape["dp"] == 2 and mesh.shape["tensor"] == 2
        )
        return fused(n, *args) if fits else local(*args)

    placed = (
        P(("groups", "dp"), "seq", "tensor"),
        P(("groups", "dp"), "seq", "tensor"),
        P(("groups", "dp"), "seq", "tensor"),
        P(("groups", "dp"), "seq"),
        P(("groups", "dp"), "seq", None),
        P("tensor", None),
    )
    return jax.shard_map(
        body,
        mesh=mesh,
        in_specs=placed,
        out_specs=(
            P(("groups", "dp"), "seq", "tensor"),
            P(("groups", "dp"), "seq", "tensor"),
            P(("groups", "dp"), "seq", "tensor"),
            P(("groups", "tensor"), None),
        ),
        check_vma=False,
    )
```

```python
import functools
import math

import jax
import jax.numpy as jnp
from jax import lax
from jax.experimental import pallas as pl
from jax.experimental.pallas import tpu as pltpu
from jax.sharding import PartitionSpec as P

HD = 64


MASKED_SCORE = -1e30


def heads_of(array):
    return array.reshape(array.shape[0], array.shape[1] // HD, HD)


def block_scores(query_block, key_block, query_utts, key_utts):
    scores = jnp.einsum(
        "qhd,khd->hqk", query_block, key_block, preferred_element_type=jnp.float32
    ) * HD ** (-0.5)
    same_utt = query_utts[:, None] == key_utts[None, :]
    return jnp.where(same_utt[None], scores, MASKED_SCORE)


def score_gradient(probs, dout_block, value_block, delta_rows):
    prob_grads = jnp.einsum(
        "qhd,khd->hqk", dout_block, value_block, preferred_element_type=jnp.float32
    )
    return (probs * (prob_grads - delta_rows[:, :, None]) * HD ** (-0.5)).astype(jnp.bfloat16)


def local(queries, key_rows, value_rows, utterance, cotangent, out_weight):
    own_queries = queries[0]
    frames_dev = own_queries.shape[0]
    width_dev = own_queries.shape[1]
    heads_dev = width_dev // HD
    query_heads = heads_of(own_queries)
    my_utts = utterance[0]
    utts_all = lax.all_gather(my_utts, "seq", axis=0, tiled=True)
    keys_all, values_all = (
        lax.all_gather(key_rows[0], "seq", axis=0, tiled=True),
        lax.all_gather(value_rows[0], "seq", axis=0, tiled=True),
    )
    frames_all = keys_all.shape[0]
    key_span = math.gcd(frames_all, 512)
    block_count = frames_all // key_span

    def key_block(block_index):
        offset = block_index * key_span
        key_block_rows = heads_of(lax.dynamic_slice_in_dim(keys_all, offset, key_span, 0))
        value_block_rows = heads_of(lax.dynamic_slice_in_dim(values_all, offset, key_span, 0))
        utt_block = lax.dynamic_slice_in_dim(utts_all, offset, key_span, 0)
        return (key_block_rows, value_block_rows, utt_block)

    def stats_step(block_index, carried):
        key_block_rows, value_block_rows, utt_block = key_block(block_index)
        running_max, running_sum = carried
        scores = block_scores(query_heads, key_block_rows, my_utts, utt_block)
        new_max = jnp.maximum(running_max, jnp.max(scores, axis=2))
        running_sum = running_sum * jnp.exp(running_max - new_max) + jnp.sum(
            jnp.exp(scores - new_max[:, :, None]), axis=2
        )
        return (new_max, running_sum)

    start_max = jnp.full((heads_dev, frames_dev), MASKED_SCORE, jnp.float32)
    start_sum = jnp.zeros((heads_dev, frames_dev), jnp.float32)
    running_max, running_sum = lax.fori_loop(0, block_count, stats_step, (start_max, start_sum))
    log_norm = running_max + jnp.log(running_sum)

    def output_step(block_index, carried):
        key_block_rows, value_block_rows, utt_block = key_block(block_index)
        scores = block_scores(query_heads, key_block_rows, my_utts, utt_block)
        probs_low = jnp.exp(scores - log_norm[:, :, None]).astype(jnp.bfloat16)
        return carried + jnp.einsum(
            "hqk,khd->hqd", probs_low, value_block_rows, preferred_element_type=jnp.float32
        )

    head_zeros = jnp.zeros((heads_dev, frames_dev, HD), jnp.float32)
    attended_acc = lax.fori_loop(0, block_count, output_step, head_zeros)
    attended = attended_acc.transpose(1, 0, 2).reshape(frames_dev, width_dev).astype(jnp.bfloat16)
    own_cot = cotangent[0]
    d_attended = lax.dot_general(
        own_cot, out_weight, (((1,), (1,)), ((), ())), preferred_element_type=jnp.float32
    ).astype(jnp.bfloat16)
    weight_term = lax.dot_general(
        attended, own_cot, (((0,), (0,)), ((), ())), preferred_element_type=jnp.float32
    )
    grad_weight = lax.psum(weight_term, ("seq", "dp"))
    dout_heads = heads_of(d_attended)
    row_delta = jnp.einsum(
        "qhd,qhd->hq", dout_heads.astype(jnp.float32), heads_of(attended).astype(jnp.float32)
    )

    def joint_step(block_index, carried):
        key_block_rows, value_block_rows, utt_block = key_block(block_index)
        query_acc_now, buffer = carried
        scores = block_scores(query_heads, key_block_rows, my_utts, utt_block)
        probs = jnp.exp(scores - log_norm[:, :, None])
        score_grads = score_gradient(probs, dout_heads, value_block_rows, row_delta)
        query_acc_now = query_acc_now + jnp.einsum(
            "hqk,khd->hqd", score_grads, key_block_rows, preferred_element_type=jnp.float32
        )
        key_part = jnp.einsum(
            "hqk,qhd->khd", score_grads, query_heads, preferred_element_type=jnp.float32
        )
        value_part = jnp.einsum(
            "hqk,qhd->khd",
            probs.astype(jnp.bfloat16),
            dout_heads,
            preferred_element_type=jnp.float32,
        )
        joined = jnp.concatenate(
            [key_part.reshape(key_span, width_dev), value_part.reshape(key_span, width_dev)], axis=1
        )
        buffer = lax.dynamic_update_slice_in_dim(buffer, joined, block_index * key_span, 0)
        return (query_acc_now, buffer)

    term_zeros = jnp.zeros((frames_all, 2 * width_dev), jnp.float32)
    query_acc, terms_all = lax.fori_loop(0, block_count, joint_step, (head_zeros, term_zeros))
    summed = lax.psum_scatter(terms_all, "seq", scatter_dimension=0, tiled=True)
    grad_key = summed[:, :width_dev].astype(jnp.bfloat16)
    grad_value = summed[:, width_dev:].astype(jnp.bfloat16)
    grad_query = query_acc.transpose(1, 0, 2).reshape(frames_dev, width_dev).astype(jnp.bfloat16)
    return (grad_query[None], grad_key[None], grad_value[None], grad_weight)


PAIR = 2 * HD
NT = (((1,), (1,)), ((), ()))
TN = (((0,), (0,)), ((), ()))
MESH = pl.DeviceIdType.MESH
CUTS = 2


def dot(a, b, dims=(((1,), (0,)), ((), ()))):
    return lax.dot_general(a, b, dims, preferred_element_type=jnp.float32)


def fused_kernel(
    n, q_ref, k_ref, v_ref, utt_ref, cot_ref, w_ref,
    dq_ref, dk_ref, dv_ref, gw_ref,
    q_all, k_all, v_all, utt_pad, utt_all, cot_all, w_own, utt_col, utt_row, probs_all, att_all,
    dq_all, dk_all, dv_all, dk_acc, dv_acc, gw_part, gw_send, gw_recv,
    local_sem, in_send, in_recv, cot_send, cot_recv, core_send, core_recv,
    out_send, out_recv, pair_send, pair_recv, gz_send, gz_recv, gx_send, gx_recv,
):
    me = lax.axis_index("seq")
    core = lax.axis_index("tensor")
    side = lax.axis_index("dp")
    rows = q_ref.shape[0]
    scale = HD ** -0.5

    def peer(d):
        return lax.rem(me + d, n)

    def frames(s):
        return pl.ds(pl.multiple_of(s * rows, rows), rows)

    def pair(s):
        return pl.ds(pl.multiple_of(s * PAIR, PAIR), PAIR)

    def slab(base, extent, who, cut):
        size = extent // (2 * CUTS)
        return pl.ds(pl.multiple_of(base + who * (extent // 2) + cut * size, size), size)

    def remote(src, dst, ssem, rsem, target):
        return pltpu.make_async_remote_copy(
            src_ref=src, dst_ref=dst, send_sem=ssem, recv_sem=rsem,
            device_id=target, device_id_type=MESH,
        )

    barrier = pltpu.get_barrier_semaphore()
    for d in range(1, n):
        pl.semaphore_signal(barrier, inc=1, device_id={"seq": peer(d)}, device_id_type=MESH)
    pl.semaphore_signal(barrier, inc=1, device_id={"tensor": 1 - core}, device_id_type=MESH)
    pl.semaphore_signal(barrier, inc=1, device_id={"dp": 1 - side}, device_id_type=MESH)

    own = pair(me)
    local_copies = [
        pltpu.make_async_copy(src, dst, local_sem.at[i])
        for i, (src, dst) in enumerate((
            (q_ref.at[:, own], q_all.at[frames(me), :]),
            (k_ref.at[:, own], k_all.at[frames(me), :]),
            (v_ref.at[:, own], v_all.at[frames(me), :]),
            (cot_ref, cot_all.at[frames(me), :]),
            (w_ref.at[own, :], w_own),
        ))
    ]
    for copy in local_copies:
        copy.start()
    utt_pad[...] = jnp.zeros_like(utt_pad)
    utt_pad[0:1, 0:rows] = utt_ref[...].astype(jnp.float32)
    utt_all[me] = utt_pad[...]

    order = [jnp.int32(0)] * (n - 1)
    count = jnp.int32(0)
    for dist in range(1, n):
        for s in (me - dist, me + dist):
            valid = jnp.logical_and(s >= 0, s < n)
            for k in range(n - 1):
                order[k] = jnp.where(jnp.logical_and(valid, count == k), s, order[k])
            count = count + valid.astype(jnp.int32)

    def onward(src, dst, s, cut, ssem, rsem, act):
        @pl.when(jnp.logical_and(s <= me, me < n - 1))
        def _():
            act(remote(src, dst, ssem.at[0, s, cut], rsem.at[s, cut], {"seq": lax.rem(me + 1, n)}))

        @pl.when(jnp.logical_and(s >= me, me > 0))
        def _():
            act(remote(src, dst, ssem.at[1, s, cut], rsem.at[s, cut], {"seq": lax.rem(me + n - 1, n)}))

    start = lambda copy: copy.start()
    wait_send = lambda copy: copy.wait_send()

    pl.semaphore_wait(barrier, n + 1)
    in_copies = []
    for d in range(1, n):
        to = {"seq": peer(d)}
        cols = pair(peer(d))
        in_copies.append(remote(utt_pad, utt_all.at[me], in_send.at[3, d], in_recv.at[3, d], to))
        for t, (src, dst) in enumerate(((k_ref, k_all), (v_ref, v_all), (q_ref, q_all))):
            in_copies.append(remote(
                src.at[:, cols], dst.at[frames(me), :], in_send.at[t, d], in_recv.at[t, d], to))

    def cot_block(s, cut):
        return cot_all.at[slab(s * rows, rows, core, cut), :]

    for cut in range(CUTS):
        onward(cot_ref.at[slab(0, rows, core, cut), :], cot_block(me, cut), me, cut,
               cot_send, cot_recv, start)
    for copy in in_copies:
        copy.start()
    for copy in local_copies:
        copy.wait()
    core_copies = []

    def take_cot(k):
        s = order[k]
        for cut in range(CUTS):
            block = cot_block(s, cut)
            copy = remote(
                block, block, core_send.at[k, cut], core_recv.at[k, cut], {"tensor": 1 - core})
            remote(block, block, core_send.at[k, cut], cot_recv.at[s, cut],
                   {"tensor": 1 - core}).wait_recv()
            onward(block, block, s, cut, cot_send, cot_recv, start)
            copy.start()
            core_copies.append(copy)

    take_cot(0)
    take_cot(1)
    for copy in in_copies:
        copy.wait_recv()

    for s in range(n):
        wide = jnp.broadcast_to(utt_all[s, 0:1, :], (128, utt_all.shape[2]))
        utt_col[s * rows:(s + 1) * rows, :] = jnp.transpose(wide)[:rows, :]
    utt_row[...] = jnp.transpose(utt_col[...])[0:8, :]

    lane = lax.broadcasted_iota(jnp.int32, (rows, PAIR), 1)
    first = lane < HD
    masks = [first.astype(jnp.float32), (lane >= HD).astype(jnp.float32)]
    masks_low = [m.astype(jnp.bfloat16) for m in masks]

    def forward(i):
        here = frames(i)
        q = q_all[here, :]
        same = utt_col[here, 0:1] == utt_row[0:1, :]
        outs = []
        for h in range(2):
            scores = dot(q * masks_low[h], k_all[...], NT) * scale
            scores = jnp.where(same, scores, MASKED_SCORE)
            e = jnp.exp(scores - jnp.max(scores, axis=1, keepdims=True))
            probs = e * (1.0 / jnp.sum(e, axis=1, keepdims=True))
            probs_all[h, here, :] = probs
            outs.append(dot(probs.astype(jnp.bfloat16), v_all[...]))
        att_all[here, :] = jnp.where(first, outs[0], outs[1]).astype(jnp.bfloat16)

    def forward_step(i, carry):
        forward(i)
        return carry

    gw_part[...] = jnp.zeros_like(gw_part)
    dk_acc[...] = jnp.zeros_like(dk_acc)
    dv_acc[...] = jnp.zeros_like(dv_acc)
    lax.fori_loop(0, n // 2, forward_step, 0)
    lax.fori_loop(n // 2, n, forward_step, 0)
    for k in range(2, n - 1):
        take_cot(k)

    def slab_half(who):
        return pl.ds(pl.multiple_of(who * HD, HD), HD)

    def weigh(i):
        here = frames(i)
        gw_part[...] += dot(att_all[here, :], cot_all[here, :], TN)

    def backward(i):
        here = frames(i)
        q = q_all[here, :]
        dout = dot(cot_all[here, :], w_own[...], NT).astype(jnp.bfloat16)
        product = dout.astype(jnp.float32) * att_all[here, :].astype(jnp.float32)
        parts = []
        for h in range(2):
            delta = jnp.sum(product * masks[h], axis=1, keepdims=True)
            dout_h = dout * masks_low[h]
            probs = probs_all[h, here, :]
            grads = (probs * (dot(dout_h, v_all[...], NT) - delta) * scale).astype(jnp.bfloat16)
            parts.append(dot(grads, k_all[...]))
            dk_acc[...] += dot(q * masks_low[h], grads, TN)
            dv_acc[...] += dot(dout_h, probs.astype(jnp.bfloat16), TN)
        dq_all[here, :] = jnp.where(first, parts[0], parts[1]).astype(jnp.bfloat16)

    out_copies = []

    def send_out(t, src, dst, to):
        d = lax.rem(to - me + n, n)
        copy = remote(
            src.at[frames(to), :], dst.at[:, own],
            out_send.at[t, d], out_recv.at[t, d], {"seq": to})
        copy.start()
        out_copies.append(copy)

    weigh(me)
    backward(me)
    for k in range(n - 1):
        for copy in core_copies[k * CUTS:(k + 1) * CUTS]:
            copy.wait_recv()
        weigh(order[k])
        if k == n - 2:
            gw_send[...] = gw_part[slab_half(1 - side), :].astype(jnp.bfloat16)
            pair_copy = remote(gw_send, gw_recv, pair_send, pair_recv, {"dp": 1 - side})
            pair_copy.start()
        backward(order[k])
        send_out(0, dq_all, dq_ref, order[k])

    dk_all[...] = jnp.transpose(dk_acc[...]).astype(jnp.bfloat16)
    dv_all[...] = jnp.transpose(dv_acc[...]).astype(jnp.bfloat16)

    gx_copies = []

    def gw_block(s, cut):
        return gw_ref.at[slab(s * PAIR, PAIR, side, cut), :]

    def pass_on(s, slot, cut):
        block = gw_block(s, cut)
        copy = remote(
            block, block, gx_send.at[slot, cut], gx_recv.at[slot, cut], {"dp": 1 - side})
        copy.start()
        gx_copies.append(copy)

    pair_copy.wait_recv()
    gw_ref[pl.ds(pl.multiple_of(me * PAIR + side * HD, HD), HD), :] = (
        gw_part[slab_half(side), :] + gw_recv[...].astype(jnp.float32)).astype(jnp.bfloat16)
    for cut in range(CUTS):
        onward(gw_block(me, cut), gw_block(me, cut), me, cut, gz_send, gz_recv, start)
    for cut in range(CUTS):
        pass_on(me, n - 1, cut)
    for t, (src, dst) in ((1, (dk_all, dk_ref)), (2, (dv_all, dv_ref))):
        for d in range(1, n):
            send_out(t, src, dst, peer(d))
    dq_ref[:, own] = dq_all[frames(me), :]
    dk_ref[:, own] = dk_all[frames(me), :]
    dv_ref[:, own] = dv_all[frames(me), :]
    for k in range(n - 1):
        s = order[k]
        for cut in range(CUTS):
            block = gw_block(s, cut)
            remote(block, block, gx_send.at[k, cut], gz_recv.at[s, cut],
                   {"dp": 1 - side}).wait_recv()
            onward(block, block, s, cut, gz_send, gz_recv, start)
            pass_on(s, k, cut)
    for copy in gx_copies + out_copies:
        copy.wait_recv()
    for s in [me] + order:
        for cut in range(CUTS):
            block, done = cot_block(s, cut), gw_block(s, cut)
            onward(block, block, s, cut, cot_send, cot_recv, wait_send)
            onward(done, done, s, cut, gz_send, gz_recv, wait_send)
    for copy in in_copies + core_copies + [pair_copy] + gx_copies + out_copies:
        copy.wait_send()


def fused(n, queries, key_rows, value_rows, utterance, cotangent, out_weight):
    rows, width = queries.shape[1:]
    depth = cotangent.shape[2]
    total = n * rows
    wide = -(-rows // 128) * 128
    low, full = jnp.bfloat16, jnp.float32
    vmem = pl.BlockSpec(memory_space=pltpu.VMEM)
    hbm = pl.BlockSpec(memory_space=pltpu.HBM)
    dma = pltpu.SemaphoreType.DMA
    dq, dk, dv, gw = pl.pallas_call(
        functools.partial(fused_kernel, n),
        out_shape=[jax.ShapeDtypeStruct((rows, width), low)] * 3
        + [jax.ShapeDtypeStruct((width, depth), low)],
        in_specs=[hbm, hbm, hbm, vmem, hbm, hbm],
        out_specs=[vmem] * 4,
        scratch_shapes=[
            pltpu.VMEM((total, PAIR), low),
            pltpu.VMEM((total, PAIR), low),
            pltpu.VMEM((total, PAIR), low),
            pltpu.VMEM((8, wide), full),
            pltpu.VMEM((n, 8, wide), full),
            pltpu.VMEM((total, depth), low),
            pltpu.VMEM((PAIR, depth), low),
            pltpu.VMEM((total, 128), full),
            pltpu.VMEM((8, total), full),
            pltpu.VMEM((2, total, total), full),
            pltpu.VMEM((total, PAIR), low),
            pltpu.VMEM((total, PAIR), low),
            pltpu.VMEM((total, PAIR), low),
            pltpu.VMEM((total, PAIR), low),
            pltpu.VMEM((PAIR, total), full),
            pltpu.VMEM((PAIR, total), full),
            pltpu.VMEM((PAIR, depth), full),
            pltpu.VMEM((HD, depth), low),
            pltpu.VMEM((HD, depth), low),
            dma((5,)), dma((4, n)), dma((4, n)), dma((2, n, CUTS)), dma((n, CUTS)),
            dma((n, CUTS)), dma((n, CUTS)), dma((3, n)), dma((3, n)), dma, dma,
            dma((2, n, CUTS)), dma((n, CUTS)), dma((n, CUTS)), dma((n, CUTS)),
        ],
        compiler_params=pltpu.CompilerParams(
            collective_id=0, has_side_effects=True, vmem_limit_bytes=60 << 20),
    )(queries[0], key_rows[0], value_rows[0], utterance, cotangent[0], out_weight)
    return dq[None], dk[None], dv[None], gw.astype(full)


def solution(mesh):
    n = mesh.shape["seq"]

    def body(*args):
        width, rows = args[0].shape[2], args[0].shape[1]
        fits = (
            width == n * PAIR and rows % (32 * CUTS) == 0 and n > 1
            and mesh.shape["dp"] == 2 and mesh.shape["tensor"] == 2
        )
        return fused(n, *args) if fits else local(*args)

    placed = (
        P(("groups", "dp"), "seq", "tensor"),
        P(("groups", "dp"), "seq", "tensor"),
        P(("groups", "dp"), "seq", "tensor"),
        P(("groups", "dp"), "seq"),
        P(("groups", "dp"), "seq", None),
        P("tensor", None),
    )
    return jax.shard_map(
        body,
        mesh=mesh,
        in_specs=placed,
        out_specs=(
            P(("groups", "dp"), "seq", "tensor"),
            P(("groups", "dp"), "seq", "tensor"),
            P(("groups", "dp"), "seq", "tensor"),
            P(("groups", "tensor"), None),
        ),
        check_vma=False,
    )
```
